32 devices in a mesh: vp: 8 (over y, x, core), ob: 4 (over z).
Axes of the slice: x: 2, y: 2, z: 4, core: 2. Of those that a mesh axis runs over, the one named last changes fastest.
Arguments:
- integrals: bfloat16 [147456, 2304], P('vp'), may hold values from -0.125 to 0.125
- amplitudes: bfloat16 [2304, 2048], P('vp', 'ob'), may hold values from -12 to 12
- rotation: bfloat16 [384, 384], replicated, may hold values from -0.3125 to 0.3125
- eps_occ: float32 [64], replicated, may hold values from -2.5 to -0.5
- eps_vir: float32 [384], replicated, may hold values from 0.2 to 4
Outputs:
- update: bfloat16 [2048, 147456], P('ob', 'vp')
The draws below stay inside these ranges and needn't reach their ends.
All inputs are finite; a program needn't handle non-finite values.
Results may differ from the reference program's by a relative error of at most 0.0058.
Values may be sent and summed in bfloat16 or wider, within the bound.
A program may use at most 192 MiB of HBM per device.

```python
import math
import jax
import jax.numpy as jnp
from jax import lax

V = 384
O = 64
AB = 147456
CDW = 2304
PAIRS = 2048


def block_scale(key, dims, cuts, smallest, high):
    level, own = 1.0, jax.random.fold_in(key, 6)
    for position, blocks in cuts:
        draws = jnp.exp(jax.random.uniform(jax.random.fold_in(own, position), (blocks,), jnp.float32, smallest / len(cuts), high / len(cuts)))
        level = level * jnp.repeat(draws, dims[position] // blocks).reshape([-1 if axis == position else 1 for axis in range(len(dims))])
    return level


def bell_draw(rng, dims, scale, most, shards=(), kind=jnp.bfloat16):
    gain = block_scale(rng, dims, shards, -0.22, 0.18) if shards else 1.0
    entries = jax.random.normal(rng, dims, jnp.float32) * scale * gain
    return jnp.minimum(jnp.maximum(entries, -most), most).astype(kind)


def setup_inputs(seed: int = 0) -> dict:
    keys = jax.random.split(jax.random.key(seed), 6)
    integrals = bell_draw(keys[0], (AB, CDW), CDW ** -0.5, 0.125, ((0, 8),))
    amplitudes = bell_draw(keys[1], (CDW, PAIRS), 2.0, 12.0, ((0, 8), (1, 4)))
    rotation = bell_draw(keys[2], (V, V), V ** -0.5, 0.3125)
    eps_occ = jnp.clip(jax.random.uniform(keys[3], (O,), jnp.float32, -2.5, -0.5), -2.5, -0.5)
    eps_vir = jnp.clip(jnp.exp(jax.random.uniform(keys[4], (V,), jnp.float32, math.log(0.2), math.log(4.0))), 0.2, 4.0)
    return dict(integrals=integrals, amplitudes=amplitudes, rotation=rotation, eps_occ=eps_occ, eps_vir=eps_vir)


def pair_energy(eps_occ, first_pair, pair_count):
    occupied = eps_occ.shape[0]
    pair_index = first_pair + jnp.arange(pair_count, dtype=jnp.int32)
    first_orbital = pair_index // occupied
    second_orbital = pair_index % occupied
    orbitals = jnp.arange(occupied, dtype=jnp.int32)
    first_energy = jnp.sum(jnp.where(orbitals[None, :] == first_orbital[:, None], eps_occ[None, :], 0.0), axis=1)
    second_energy = jnp.sum(jnp.where(orbitals[None, :] == second_orbital[:, None], eps_occ[None, :], 0.0), axis=1)
    return first_energy + second_energy


def dress_pairs(ladder, rotation, eps_occ, eps_vir, first_pair):
    pair_count = ladder.shape[0]
    orbital_count = rotation.shape[0]
    half = jnp.dot(ladder.reshape(pair_count * orbital_count, orbital_count), rotation, preferred_element_type=jnp.float32)
    half = half.astype(jnp.bfloat16).reshape(pair_count, orbital_count, orbital_count)
    dressed = jnp.einsum("af,nae->nfe", rotation.astype(jnp.float32), half.astype(jnp.float32))
    energy = pair_energy(eps_occ, first_pair, pair_count)
    divisor = energy[:, None, None] - eps_vir[None, :, None] - eps_vir[None, None, :]
    return (dressed / divisor).astype(jnp.bfloat16).reshape(pair_count, orbital_count * orbital_count)


def reference(integrals, amplitudes, rotation, eps_occ, eps_vir):
    block_size = 32

    def one_block(block_index):
        offset = (block_index * block_size).astype(jnp.int32)
        panels = lax.dynamic_slice_in_dim(amplitudes, offset, block_size, 1)
        ladder = lax.dot_general(panels, integrals, (((0,), (1,)), ((), ())), preferred_element_type=jnp.float32)
        ladder = ladder.astype(jnp.bfloat16)
        return dress_pairs(ladder, rotation, eps_occ, eps_vir, offset)

    blocks = lax.map(one_block, jnp.arange(PAIRS // block_size, dtype=jnp.int32))
    return blocks.reshape(PAIRS, V * V)
```

```python
import functools

import jax
import jax.numpy as jnp
from jax import lax
from jax.experimental import pallas as pl
from jax.experimental.pallas import tpu as pltpu
from jax.sharding import PartitionSpec as P

LANES = 128
ROWS = 16
SLOTS = 3


def pair_energy(eps_occ, first_pair, pair_count):
    occupied = eps_occ.shape[0]
    pair_index = first_pair + jnp.arange(pair_count, dtype=jnp.int32)
    first_orbital = pair_index // occupied
    second_orbital = pair_index % occupied
    orbitals = jnp.arange(occupied, dtype=jnp.int32)
    first_energy = jnp.sum(
        jnp.where(orbitals[None, :] == first_orbital[:, None], eps_occ[None, :], 0.0), axis=1
    )
    second_energy = jnp.sum(
        jnp.where(orbitals[None, :] == second_orbital[:, None], eps_occ[None, :], 0.0), axis=1
    )
    return first_energy + second_energy


def ladder_kernel(
    peers,
    gather,
    amplitudes,
    integrals,
    rotation,
    rotation_t,
    energy,
    eps_column,
    eps_row,
    out,
    landed,
    panels,
    tiles,
    spread,
    sending,
    halves,
    dressed,
    updates,
    packed,
    panel_send,
    panel_recv,
    own_sem,
    tile_sem,
    half_send,
    half_recv,
    load_sem,
    update_send,
    update_recv,
):
    chunks, _, width = amplitudes.shape
    row_count, summed = integrals.shape
    orbitals = rotation.shape[0]
    _, groups, per_owner, group_rows, _ = landed.shape
    chunk_pairs = per_owner // chunks
    first_rows = row_count // orbitals
    strips = orbitals // LANES
    batches = per_owner // ROWS
    per_chunk = batches // chunks
    steps = chunks * first_rows
    me = lax.axis_index("vp")

    def peer_of(step):
        return lax.rem(me + step, peers)

    def each_peer(body):
        def run(step, carry):
            body(step, peer_of(step))
            return carry

        lax.fori_loop(1, peers, run, 0)

    barrier = pltpu.get_barrier_semaphore()
    each_peer(lambda step, peer: pl.semaphore_signal(barrier, inc=1, device_id={"vp": peer}))

    def fetch(step):
        first = pl.multiple_of(lax.rem(step, first_rows) * orbitals, orbitals)
        slot = lax.rem(step, SLOTS)
        return pltpu.make_async_copy(
            integrals.at[pl.ds(first, orbitals)], tiles.at[slot], tile_sem.at[slot]
        )

    for step in range(min(SLOTS - 1, steps)):
        fetch(step).start()
    pl.semaphore_wait(barrier, peers - 1)

    def panel_copy(chunk, step, peer, origin):
        return pltpu.make_async_remote_copy(
            src_ref=amplitudes.at[chunk],
            dst_ref=panels.at[chunk, origin],
            send_sem=panel_send.at[chunk, step],
            recv_sem=panel_recv.at[chunk, origin],
            device_id={"vp": peer},
        )

    def own_panel(chunk):
        return pltpu.make_async_copy(
            amplitudes.at[chunk], panels.at[chunk, me if gather else 0], own_sem
        )

    for chunk in range(chunks):
        if gather:
            each_peer(lambda step, peer: panel_copy(chunk, step, peer, me).start())
        own_panel(chunk).start()
        own_panel(chunk).wait()
        if gather and chunk == 0:
            each_peer(lambda step, peer: panel_copy(0, step, peer, peer).wait_recv())

    def half_copy(turn, step, peer, origin):
        chunk, group = lax.div(turn, groups), lax.rem(turn, groups)
        slot = lax.rem(turn, 2)
        return pltpu.make_async_remote_copy(
            src_ref=sending.at[slot, pl.ds(peer * chunk_pairs, chunk_pairs)],
            dst_ref=landed.at[origin, group, pl.ds(chunk * chunk_pairs, chunk_pairs)],
            send_sem=half_send.at[slot, step],
            recv_sem=half_recv.at[turn, origin],
            device_id={"vp": peer},
        )

    def send_turn(turn, carry):
        chunk, group = lax.div(turn, groups), lax.rem(turn, groups)
        slot = lax.rem(turn, 2)
        if gather:
            for later in range(1, chunks):

                @pl.when(turn == later * groups)
                def _():
                    each_peer(lambda step, peer: panel_copy(later, step, peer, peer).wait_recv())

        def one_row(row, carry):
            step = turn * group_rows + row
            fetch(step).wait()

            @pl.when(step + (SLOTS - 1) < steps)
            def _():
                fetch(step + (SLOTS - 1)).start()

            ladder = jnp.dot(
                tiles[lax.rem(step, SLOTS)],
                panels[chunk].reshape(summed, width),
                preferred_element_type=jnp.float32,
            )
            half = jnp.dot(
                ladder.T.astype(jnp.bfloat16), rotation[...], preferred_element_type=jnp.float32
            )
            for strip in range(strips):
                spread[strip, pl.ds(row, width, stride=group_rows), :] = half[
                    :, strip * LANES : (strip + 1) * LANES
                ]
            return carry

        lax.fori_loop(0, group_rows, one_row, 0)

        @pl.when(turn >= 2)
        def _():
            each_peer(lambda step, peer: half_copy(turn - 2, step, peer, me).wait_send())

        def narrow(pair, carry):
            first = pl.multiple_of(pair * group_rows, group_rows)
            for strip in range(strips):
                sending[slot, pair, :, pl.ds(strip * LANES, LANES)] = spread[
                    strip, pl.ds(first, group_rows), :
                ].astype(jnp.bfloat16)
            return carry

        lax.fori_loop(0, width, narrow, 0, unroll=8)
        each_peer(lambda step, peer: half_copy(turn, step, peer, me).start())
        own = pltpu.make_async_copy(
            sending.at[slot, pl.ds(me * chunk_pairs, chunk_pairs)],
            landed.at[me, group, pl.ds(chunk * chunk_pairs, chunk_pairs)],
            own_sem,
        )
        own.start()
        own.wait()
        return carry

    turns = chunks * groups
    lax.fori_loop(0, turns, send_turn, 0)

    def update_copy(batch, step, peer, origin):
        slot = lax.rem(batch, 2)
        return pltpu.make_async_remote_copy(
            src_ref=updates.at[slot, :, pl.ds(pl.multiple_of(peer * row_count, LANES), row_count)],
            dst_ref=out.at[pl.ds(pl.multiple_of(origin * per_owner + batch * ROWS, ROWS), ROWS)],
            send_sem=update_send.at[slot, step],
            recv_sem=update_recv.at[batch, origin],
            device_id={"vp": peer},
        )

    def return_batch(batch, carry):
        slot = lax.rem(batch, 2)
        chunk = lax.div(batch, per_chunk)

        @pl.when(lax.rem(batch, per_chunk) == 0)
        def _():
            def arrived(group, carry):
                each_peer(
                    lambda step, peer: half_copy(
                        chunk * groups + group, step, peer, peer
                    ).wait_recv()
                )
                return carry

            lax.fori_loop(0, groups, arrived, 0)

        load = pltpu.make_async_copy(
            landed.at[:, :, pl.ds(batch * ROWS, ROWS)], halves, load_sem
        )
        load.start()
        load.wait()

        def one_pair(pair, carry):
            if group_rows % ROWS == 0:
                half = halves[:, :, pair].reshape(orbitals, orbitals)
            else:
                for origin in range(peers):
                    for group in range(groups):
                        packed[pl.ds((origin * groups + group) * group_rows, group_rows), :] = (
                            halves[origin, group, pair].astype(jnp.float32)
                        )
                half = packed[...].astype(jnp.bfloat16)
            full = jnp.dot(rotation_t[...], half, preferred_element_type=jnp.float32)
            divisor = energy[batch * ROWS + pair] - eps_column[...] - eps_row[...]
            full = full / divisor
            first = pl.multiple_of(pair * orbitals, orbitals)
            for strip in range(strips):
                dressed[strip, pl.ds(first, orbitals), :] = full[
                    :, strip * LANES : (strip + 1) * LANES
                ]
            return carry

        lax.fori_loop(0, ROWS, one_pair, 0)

        @pl.when(batch >= 2)
        def _():
            each_peer(lambda step, peer: update_copy(batch - 2, step, peer, me).wait_send())

        def lay_out(orbital, carry):
            for strip in range(strips):
                column = pl.multiple_of(orbital * orbitals + strip * LANES, LANES)
                updates[slot, :, pl.ds(column, LANES)] = dressed[
                    strip, pl.ds(orbital, ROWS, stride=orbitals), :
                ].astype(jnp.bfloat16)
            return carry

        lax.fori_loop(0, orbitals, lay_out, 0, unroll=8)
        each_peer(lambda step, peer: update_copy(batch, step, peer, me).start())
        own = pltpu.make_async_copy(
            updates.at[slot, :, pl.ds(pl.multiple_of(me * row_count, LANES), row_count)],
            out.at[pl.ds(pl.multiple_of(me * per_owner + batch * ROWS, ROWS), ROWS)],
            own_sem,
        )
        own.start()
        own.wait()
        return carry

    lax.fori_loop(0, batches, return_batch, 0)

    if gather:
        for chunk in range(chunks):
            each_peer(lambda step, peer: panel_copy(chunk, step, peer, me).wait_send())
    for turn in range(max(0, turns - 2), turns):
        each_peer(lambda step, peer: half_copy(turn, step, peer, me).wait_send())
    for batch in range(max(0, batches - 2), batches):
        each_peer(lambda step, peer: update_copy(batch, step, peer, me).wait_send())

    def all_arrived(batch, carry):
        each_peer(lambda step, peer: update_copy(batch, step, peer, peer).wait_recv())
        return carry

    lax.fori_loop(0, batches, all_arrived, 0)


def shards(integrals, amplitudes, rotation, eps_occ, eps_vir):
    row_count, summed = integrals.shape
    depth, pair_count = amplitudes.shape
    orbitals = rotation.shape[0]
    peers = lax.axis_size("vp")
    per_owner = pair_count // peers
    first_rows = row_count // orbitals
    group_rows = ROWS if first_rows % ROWS == 0 else first_rows
    groups = first_rows // group_rows
    chunks = 2 if per_owner % (2 * ROWS) == 0 else 1
    chunk_pairs = per_owner // chunks
    width = peers * chunk_pairs
    batches = per_owner // ROWS
    turns = chunks * groups
    gather = depth % ROWS == 0
    if not gather:
        amplitudes = lax.all_gather(amplitudes, "vp", axis=0, tiled=True)
        depth = summed
    amplitudes = (
        amplitudes.reshape(depth, peers, chunks, chunk_pairs)
        .transpose(2, 0, 1, 3)
        .reshape(chunks, depth, width)
    )
    first_pair = lax.axis_index("ob") * pair_count + lax.axis_index("vp") * per_owner
    energy = pair_energy(eps_occ, first_pair, per_owner)
    bf16, f32 = jnp.bfloat16, jnp.float32
    vmem = pl.BlockSpec(memory_space=pltpu.VMEM)
    anywhere = pl.BlockSpec(memory_space=pl.ANY)
    spare = (LANES, LANES) if group_rows % ROWS == 0 else (orbitals, orbitals)
    flops = 2 * row_count * summed * pair_count + 4 * pair_count * row_count * orbitals
    result, _ = pl.pallas_call(
        functools.partial(ladder_kernel, peers, gather),
        out_shape=(
            jax.ShapeDtypeStruct((pair_count, row_count), bf16),
            jax.ShapeDtypeStruct((peers, groups, per_owner, group_rows, orbitals), bf16),
        ),
        in_specs=[
            anywhere,
            anywhere,
            vmem,
            vmem,
            pl.BlockSpec(memory_space=pltpu.SMEM),
            vmem,
            vmem,
        ],
        out_specs=(anywhere, anywhere),
        scratch_shapes=[
            pltpu.VMEM((chunks, summed // depth, depth, width), bf16),
            pltpu.VMEM((SLOTS, orbitals, summed), bf16),
            pltpu.VMEM((orbitals // LANES, width * group_rows, LANES), f32),
            pltpu.VMEM((2, width, group_rows, orbitals), bf16),
            pltpu.VMEM((peers, groups, ROWS, group_rows, orbitals), bf16),
            pltpu.VMEM((orbitals // LANES, ROWS * orbitals, LANES), f32),
            pltpu.VMEM((2, ROWS, orbitals * orbitals), bf16),
            pltpu.VMEM(spare, f32),
            pltpu.SemaphoreType.DMA((chunks, peers)),
            pltpu.SemaphoreType.DMA((chunks, peers)),
            pltpu.SemaphoreType.DMA,
            pltpu.SemaphoreType.DMA((SLOTS,)),
            pltpu.SemaphoreType.DMA((2, peers)),
            pltpu.SemaphoreType.DMA((turns, peers)),
            pltpu.SemaphoreType.DMA,
            pltpu.SemaphoreType.DMA((2, peers)),
            pltpu.SemaphoreType.DMA((batches, peers)),
        ],
        cost_estimate=pl.CostEstimate(
            flops=flops, bytes_accessed=chunks * 2 * row_count * summed, transcendentals=0
        ),
        compiler_params=pltpu.CompilerParams(
            collective_id=0, has_side_effects=True, vmem_limit_bytes=60 * 1024 * 1024
        ),
    )(
        amplitudes,
        integrals,
        rotation,
        rotation.T,
        energy,
        eps_vir.reshape(orbitals, 1),
        eps_vir.reshape(1, orbitals),
    )
    return result


def solution(mesh):
    return jax.shard_map(
        shards,
        mesh=mesh,
        in_specs=(P("vp", None), P("vp", "ob"), P(), P(), P()),
        out_specs=P("ob", "vp"),
        check_vma=False,
    )
```

```python
import functools

import jax
import jax.numpy as jnp
from jax import lax
from jax.experimental import pallas as pl
from jax.experimental.pallas import tpu as pltpu
from jax.sharding import PartitionSpec as P

LANES = 128
ROWS = 16
SLOTS = 3


def ladder_kernel(
    peers,
    gather,
    amplitudes,
    integrals,
    rotation,
    eps_occ,
    eps_vir,
    out,
    landed,
    panels,
    tiles,
    spread,
    sending,
    halves,
    dressed,
    updates,
    packed,
    rotation_t,
    eps_first,
    panel_send,
    panel_recv,
    own_sem,
    tile_sem,
    half_send,
    half_recv,
    load_sem,
    update_send,
    update_recv,
):
    chunks, _, _, width = panels.shape
    pair_count = amplitudes.shape[1]
    row_count, summed = integrals.shape
    orbitals, occupied = rotation.shape[0], eps_occ.shape[0]
    _, groups, per_owner, group_rows, _ = landed.shape
    chunk_pairs = per_owner // chunks
    first_rows = row_count // orbitals
    strips = orbitals // LANES
    batches = per_owner // ROWS
    per_chunk = batches // chunks
    steps = chunks * first_rows
    me = lax.axis_index("vp")

    def peer_of(step):
        return lax.rem(me + step, peers)

    def each_peer(body):
        def run(step, carry):
            body(step, peer_of(step))
            return carry

        lax.fori_loop(1, peers, run, 0)

    barrier = pltpu.get_barrier_semaphore()
    each_peer(lambda step, peer: pl.semaphore_signal(barrier, inc=1, device_id={"vp": peer}))

    def fetch(step):
        first = pl.multiple_of(lax.rem(step, first_rows) * orbitals, orbitals)
        slot = lax.rem(step, SLOTS)
        return pltpu.make_async_copy(
            integrals.at[pl.ds(first, orbitals)], tiles.at[slot], tile_sem.at[slot]
        )

    for step in range(min(SLOTS - 1, steps)):
        fetch(step).start()
    pl.semaphore_wait(barrier, peers - 1)

    sibling = me + 1 - 2 * lax.rem(me, 2)

    def own_columns(chunk):
        return amplitudes.at[:, pl.ds(chunk * width, width)]

    def panel_copy(chunk, index, peer, origin, hand_on):
        return pltpu.make_async_remote_copy(
            src_ref=panels.at[chunk, origin] if hand_on else own_columns(chunk),
            dst_ref=panels.at[chunk, origin],
            send_sem=panel_send.at[chunk, index],
            recv_sem=panel_recv.at[chunk, origin],
            device_id={"vp": peer},
        )

    def start_panels(chunk):
        if gather:
            for step in range(2, peers, 2):
                panel_copy(chunk, step, peer_of(step), me, False).start()
            panel_copy(chunk, 1, sibling, me, False).start()
        own = pltpu.make_async_copy(
            own_columns(chunk), panels.at[chunk, me if gather else 0], own_sem
        )
        own.start()
        own.wait()

    def finish_panels(chunk):
        for step in range(2, peers, 2):
            panel_copy(chunk, step, sibling, peer_of(step), True).wait_recv()
            panel_copy(chunk, step + 1, sibling, peer_of(step), True).start()
        for step in range(0, peers, 2):
            panel_copy(chunk, 1, sibling, lax.rem(sibling + step, peers), True).wait_recv()

    start_panels(0)
    rotation_t[...] = rotation[...].T
    eps_first[...] = jnp.broadcast_to(eps_vir[...].reshape(1, orbitals), (orbitals, orbitals)).T
    if gather:
        finish_panels(0)
    for chunk in range(1, chunks):
        start_panels(chunk)

    def half_copy(turn, step, peer, origin):
        chunk, group = lax.div(turn, groups), lax.rem(turn, groups)
        slot = lax.rem(turn, 2)
        return pltpu.make_async_remote_copy(
            src_ref=sending.at[slot, pl.ds(peer * chunk_pairs, chunk_pairs)],
            dst_ref=landed.at[origin, group, pl.ds(chunk * chunk_pairs, chunk_pairs)],
            send_sem=half_send.at[slot, step],
            recv_sem=half_recv.at[turn, origin],
            device_id={"vp": peer},
        )

    def send_turn(turn, carry):
        chunk, group = lax.div(turn, groups), lax.rem(turn, groups)
        slot = lax.rem(turn, 2)
        if gather:
            for later in range(1, chunks):

                @pl.when(turn == later * groups)
                def _():
                    finish_panels(later)

        def one_row(row, carry):
            step = turn * group_rows + row
            fetch(step).wait()

            @pl.when(step + (SLOTS - 1) < steps)
            def _():
                fetch(step + (SLOTS - 1)).start()

            ladder = jnp.dot(
                tiles[lax.rem(step, SLOTS)],
                panels[chunk].reshape(summed, width),
                preferred_element_type=jnp.float32,
            )
            half = jnp.dot(
                ladder.T.astype(jnp.bfloat16), rotation[...], preferred_element_type=jnp.float32
            )
            for strip in range(strips):
                spread[strip, pl.ds(row, width, stride=group_rows), :] = half[
                    :, strip * LANES : (strip + 1) * LANES
                ]
            return carry

        lax.fori_loop(0, group_rows, one_row, 0)

        @pl.when(turn >= 2)
        def _():
            each_peer(lambda step, peer: half_copy(turn - 2, step, peer, me).wait_send())

        def narrow(pair, carry):
            first = pl.multiple_of(pair * group_rows, group_rows)
            for strip in range(strips):
                sending[slot, pair, :, pl.ds(strip * LANES, LANES)] = spread[
                    strip, pl.ds(first, group_rows), :
                ].astype(jnp.bfloat16)
            return carry

        lax.fori_loop(0, width, narrow, 0, unroll=8)
        each_peer(lambda step, peer: half_copy(turn, step, peer, me).start())
        own = pltpu.make_async_copy(
            sending.at[slot, pl.ds(me * chunk_pairs, chunk_pairs)],
            landed.at[me, group, pl.ds(chunk * chunk_pairs, chunk_pairs)],
            own_sem,
        )
        own.start()
        own.wait()
        return carry

    turns = chunks * groups
    lax.fori_loop(0, turns, send_turn, 0)

    def first_row(batch, origin):
        chunk, part = lax.div(batch, per_chunk), lax.rem(batch, per_chunk)
        return pl.multiple_of(chunk * width + origin * chunk_pairs + part * ROWS, ROWS)

    def update_copy(batch, step, peer, origin):
        slot = lax.rem(batch, 2)
        return pltpu.make_async_remote_copy(
            src_ref=updates.at[slot, :, pl.ds(pl.multiple_of(peer * row_count, LANES), row_count)],
            dst_ref=out.at[pl.ds(first_row(batch, origin), ROWS)],
            send_sem=update_send.at[slot, step],
            recv_sem=update_recv.at[batch, origin],
            device_id={"vp": peer},
        )

    def return_batch(batch, carry):
        slot = lax.rem(batch, 2)
        chunk = lax.div(batch, per_chunk)

        @pl.when(lax.rem(batch, per_chunk) == 0)
        def _():
            def arrived(group, carry):
                each_peer(
                    lambda step, peer: half_copy(
                        chunk * groups + group, step, peer, peer
                    ).wait_recv()
                )
                return carry

            lax.fori_loop(0, groups, arrived, 0)

        load = pltpu.make_async_copy(
            landed.at[:, :, pl.ds(batch * ROWS, ROWS)], halves, load_sem
        )
        load.start()
        load.wait()

        def one_pair(pair, carry):
            if group_rows % ROWS == 0:
                half = halves[:, :, pair].reshape(orbitals, orbitals)
            else:
                for origin in range(peers):
                    for group in range(groups):
                        packed[pl.ds((origin * groups + group) * group_rows, group_rows), :] = (
                            halves[origin, group, pair].astype(jnp.float32)
                        )
                half = packed[...].astype(jnp.bfloat16)
            full = jnp.dot(rotation_t[...], half, preferred_element_type=jnp.float32)
            index = lax.axis_index("ob") * pair_count + first_row(batch, me) + pair
            energy = eps_occ[lax.div(index, occupied)] + eps_occ[lax.rem(index, occupied)]
            divisor = energy - eps_first[...] - eps_vir[...].reshape(1, orbitals)
            full = full / divisor
            first = pl.multiple_of(pair * orbitals, orbitals)
            for strip in range(strips):
                dressed[strip, pl.ds(first, orbitals), :] = full[
                    :, strip * LANES : (strip + 1) * LANES
                ]
            return carry

        lax.fori_loop(0, ROWS, one_pair, 0)

        @pl.when(batch >= 2)
        def _():
            each_peer(lambda step, peer: update_copy(batch - 2, step, peer, me).wait_send())

        def lay_out(orbital, carry):
            for strip in range(strips):
                column = pl.multiple_of(orbital * orbitals + strip * LANES, LANES)
                updates[slot, :, pl.ds(column, LANES)] = dressed[
                    strip, pl.ds(orbital, ROWS, stride=orbitals), :
                ].astype(jnp.bfloat16)
            return carry

        lax.fori_loop(0, orbitals, lay_out, 0, unroll=8)
        each_peer(lambda step, peer: update_copy(batch, step, peer, me).start())
        own = pltpu.make_async_copy(
            updates.at[slot, :, pl.ds(pl.multiple_of(me * row_count, LANES), row_count)],
            out.at[pl.ds(first_row(batch, me), ROWS)],
            own_sem,
        )
        own.start()
        own.wait()
        return carry

    lax.fori_loop(0, batches, return_batch, 0)

    if gather:
        for chunk in range(chunks):
            each_peer(lambda step, peer: panel_copy(chunk, step, sibling, me, False).wait_send())
    for turn in range(max(0, turns - 2), turns):
        each_peer(lambda step, peer: half_copy(turn, step, peer, me).wait_send())
    for batch in range(max(0, batches - 2), batches):
        each_peer(lambda step, peer: update_copy(batch, step, peer, me).wait_send())

    def all_arrived(batch, carry):
        each_peer(lambda step, peer: update_copy(batch, step, peer, peer).wait_recv())
        return carry

    lax.fori_loop(0, batches, all_arrived, 0)


def copy_kernel(source, target):
    target[...] = source[...]


def shards(integrals, amplitudes, rotation, eps_occ, eps_vir):
    row_count, summed = integrals.shape
    depth, pair_count = amplitudes.shape
    orbitals = rotation.shape[0]
    peers = lax.axis_size("vp")
    per_owner = pair_count // peers
    first_rows = row_count // orbitals
    group_rows = ROWS if first_rows % ROWS == 0 else first_rows
    groups = first_rows // group_rows
    chunks = 2 if per_owner % (2 * ROWS) == 0 else 1
    chunk_pairs = per_owner // chunks
    width = peers * chunk_pairs
    batches = per_owner // ROWS
    turns = chunks * groups
    gather = depth % ROWS == 0 and peers % 2 == 0
    if not gather:
        amplitudes = lax.all_gather(amplitudes, "vp", axis=0, tiled=True)
        depth = summed
    bf16, f32 = jnp.bfloat16, jnp.float32
    vmem = pl.BlockSpec(memory_space=pltpu.VMEM)
    anywhere = pl.BlockSpec(memory_space=pl.ANY)
    spare = (LANES, LANES) if group_rows % ROWS == 0 else (orbitals, orbitals)
    flops = 2 * row_count * summed * pair_count + 4 * pair_count * row_count * orbitals
    result, _ = pl.pallas_call(
        functools.partial(ladder_kernel, peers, gather),
        out_shape=(
            jax.ShapeDtypeStruct((pair_count, row_count), bf16),
            jax.ShapeDtypeStruct((peers, groups, per_owner, group_rows, orbitals), bf16),
        ),
        in_specs=[
            anywhere,
            anywhere,
            vmem,
            pl.BlockSpec(memory_space=pltpu.SMEM),
            vmem,
        ],
        out_specs=(anywhere, anywhere),
        scratch_shapes=[
            pltpu.VMEM((chunks, summed // depth, depth, width), bf16),
            pltpu.VMEM((SLOTS, orbitals, summed), bf16),
            pltpu.VMEM((orbitals // LANES, width * group_rows, LANES), f32),
            pltpu.VMEM((2, width, group_rows, orbitals), bf16),
            pltpu.VMEM((peers, groups, ROWS, group_rows, orbitals), bf16),
            pltpu.VMEM((orbitals // LANES, ROWS * orbitals, LANES), f32),
            pltpu.VMEM((2, ROWS, orbitals * orbitals), bf16),
            pltpu.VMEM(spare, f32),
            pltpu.VMEM((orbitals, orbitals), bf16),
            pltpu.VMEM((orbitals, orbitals), f32),
            pltpu.SemaphoreType.DMA((chunks, peers)),
            pltpu.SemaphoreType.DMA((chunks, peers)),
            pltpu.SemaphoreType.DMA,
            pltpu.SemaphoreType.DMA((SLOTS,)),
            pltpu.SemaphoreType.DMA((2, peers)),
            pltpu.SemaphoreType.DMA((turns, peers)),
            pltpu.SemaphoreType.DMA,
            pltpu.SemaphoreType.DMA((2, peers)),
            pltpu.SemaphoreType.DMA((batches, peers)),
        ],
        cost_estimate=pl.CostEstimate(
            flops=flops, bytes_accessed=chunks * 2 * row_count * summed, transcendentals=0
        ),
        compiler_params=pltpu.CompilerParams(
            collective_id=0, has_side_effects=True, vmem_limit_bytes=60 * 1024 * 1024
        ),
    )(amplitudes, integrals, rotation, eps_occ, eps_vir)
    block = pl.BlockSpec((2 * ROWS, row_count), lambda step: (step, 0))
    return pl.pallas_call(
        copy_kernel,
        out_shape=jax.ShapeDtypeStruct(result.shape, bf16),
        grid=(pair_count // (2 * ROWS),),
        in_specs=[block],
        out_specs=block,
        cost_estimate=pl.CostEstimate(
            flops=0, bytes_accessed=4 * pair_count * row_count, transcendentals=0
        ),
        compiler_params=pltpu.CompilerParams(vmem_limit_bytes=60 * 1024 * 1024),
    )(result)


def solution(mesh):
    return jax.shard_map(
        shards,
        mesh=mesh,
        in_specs=(P("vp", None), P("vp", "ob"), P(), P(), P()),
        out_specs=P("ob", "vp"),
        check_vma=False,
    )
```

```python
import functools

import jax
import jax.numpy as jnp
from jax import lax
from jax.experimental import pallas as pl
from jax.experimental.pallas import tpu as pltpu
from jax.sharding import PartitionSpec as P

LANES = 128
ROWS = 16
SLOTS = 6


def ladder_kernel(
    peers,
    gather,
    amplitudes,
    integrals,
    rotation,
    eps_occ,
    eps_vir,
    out,
    landed,
    panels,
    tiles,
    spread,
    sending,
    halves,
    updates,
    packed,
    rotation_t,
    eps_first,
    panel_send,
    panel_recv,
    own_sem,
    tile_sem,
    half_send,
    half_recv,
    load_sem,
    update_send,
    update_recv,
):
    chunks, _, _, width = panels.shape
    pair_count = amplitudes.shape[1]
    row_count, summed = integrals.shape
    orbitals, occupied = rotation.shape[0], eps_occ.shape[0]
    _, groups, per_owner, group_rows, _ = landed.shape
    chunk_pairs = per_owner // chunks
    first_rows = row_count // orbitals
    strips = orbitals // LANES
    batches = per_owner // ROWS
    per_chunk = batches // chunks
    steps = chunks * first_rows
    me = lax.axis_index("vp")

    def peer_of(step):
        return lax.rem(me + step, peers)

    def each_peer(body):
        def run(step, carry):
            body(step, peer_of(step))
            return carry

        lax.fori_loop(1, peers, run, 0)

    barrier = pltpu.get_barrier_semaphore()
    each_peer(lambda step, peer: pl.semaphore_signal(barrier, inc=1, device_id={"vp": peer}))

    def fetch(step):
        first = pl.multiple_of(lax.rem(step, first_rows) * orbitals, orbitals)
        slot = lax.rem(step, SLOTS)
        return pltpu.make_async_copy(
            integrals.at[pl.ds(first, orbitals)], tiles.at[slot], tile_sem.at[slot]
        )

    for step in range(min(SLOTS - 1, steps)):
        fetch(step).start()
    pl.semaphore_wait(barrier, peers - 1)

    sibling = me + 1 - 2 * lax.rem(me, 2)

    def own_columns(chunk):
        return amplitudes.at[:, pl.ds(chunk * width, width)]

    def panel_copy(chunk, index, peer, origin, hand_on):
        return pltpu.make_async_remote_copy(
            src_ref=panels.at[chunk, origin] if hand_on else own_columns(chunk),
            dst_ref=panels.at[chunk, origin],
            send_sem=panel_send.at[chunk, index],
            recv_sem=panel_recv.at[chunk, origin],
            device_id={"vp": peer},
        )

    def start_panels(chunk):
        if gather:
            for step in range(2, peers, 2):
                panel_copy(chunk, step, peer_of(step), me, False).start()
            panel_copy(chunk, 1, sibling, me, False).start()
        own = pltpu.make_async_copy(
            own_columns(chunk), panels.at[chunk, me if gather else 0], own_sem
        )
        own.start()
        own.wait()

    def finish_panels(chunk):
        for step in range(2, peers, 2):
            panel_copy(chunk, step, sibling, peer_of(step), True).wait_recv()
            panel_copy(chunk, step + 1, sibling, peer_of(step), True).start()
        for step in range(0, peers, 2):
            panel_copy(chunk, 1, sibling, lax.rem(sibling + step, peers), True).wait_recv()

    start_panels(0)
    rotation_t[...] = rotation[...].T
    eps_first[...] = jnp.broadcast_to(eps_vir[...].reshape(1, orbitals), (orbitals, orbitals)).T
    if gather:
        finish_panels(0)
    for chunk in range(1, chunks):
        start_panels(chunk)

    def half_copy(turn, step, peer, origin):
        chunk, group = lax.div(turn, groups), lax.rem(turn, groups)
        slot = lax.rem(turn, 2)
        return pltpu.make_async_remote_copy(
            src_ref=sending.at[slot, pl.ds(peer * chunk_pairs, chunk_pairs)],
            dst_ref=landed.at[origin, group, pl.ds(chunk * chunk_pairs, chunk_pairs)],
            send_sem=half_send.at[slot, step],
            recv_sem=half_recv.at[turn, origin],
            device_id={"vp": peer},
        )

    def send_turn(turn, carry):
        chunk, group = lax.div(turn, groups), lax.rem(turn, groups)
        slot = lax.rem(turn, 2)
        if gather:
            for later in range(1, chunks):

                @pl.when(turn == later * groups)
                def _():
                    finish_panels(later)

        def one_row(row, carry):
            step = turn * group_rows + row
            fetch(step).wait()

            @pl.when(step + (SLOTS - 1) < steps)
            def _():
                fetch(step + (SLOTS - 1)).start()

            ladder = jnp.dot(
                tiles[lax.rem(step, SLOTS)],
                panels[chunk].reshape(summed, width),
                preferred_element_type=jnp.float32,
            )
            half = jnp.dot(
                ladder.T.astype(jnp.bfloat16), rotation[...], preferred_element_type=jnp.float32
            )
            for strip in range(strips):
                spread[strip, pl.ds(row, width, stride=group_rows), :] = half[
                    :, strip * LANES : (strip + 1) * LANES
                ]
            return carry

        lax.fori_loop(0, group_rows, one_row, 0)

        @pl.when(turn >= 2)
        def _():
            each_peer(lambda step, peer: half_copy(turn - 2, step, peer, me).wait_send())

        def narrow(pair, carry):
            first = pl.multiple_of(pair * group_rows, group_rows)
            for strip in range(strips):
                sending[slot, pair, :, pl.ds(strip * LANES, LANES)] = spread[
                    strip, pl.ds(first, group_rows), :
                ].astype(jnp.bfloat16)
            return carry

        lax.fori_loop(0, width, narrow, 0, unroll=8)
        each_peer(lambda step, peer: half_copy(turn, step, peer, me).start())
        own = pltpu.make_async_copy(
            sending.at[slot, pl.ds(me * chunk_pairs, chunk_pairs)],
            landed.at[me, group, pl.ds(chunk * chunk_pairs, chunk_pairs)],
            own_sem,
        )
        own.start()
        own.wait()
        return carry

    turns = chunks * groups
    lax.fori_loop(0, turns, send_turn, 0)

    def first_row(batch, origin):
        chunk, part = lax.div(batch, per_chunk), lax.rem(batch, per_chunk)
        return pl.multiple_of(chunk * width + origin * chunk_pairs + part * ROWS, ROWS)

    def update_copy(batch, step, peer, origin):
        slot = lax.rem(batch, 2)
        return pltpu.make_async_remote_copy(
            src_ref=updates.at[slot, :, pl.ds(pl.multiple_of(peer * row_count, LANES), row_count)],
            dst_ref=out.at[pl.ds(first_row(batch, origin), ROWS)],
            send_sem=update_send.at[slot, step],
            recv_sem=update_recv.at[batch, origin],
            device_id={"vp": peer},
        )

    def return_batch(batch, carry):
        slot = lax.rem(batch, 2)
        chunk = lax.div(batch, per_chunk)

        @pl.when(lax.rem(batch, per_chunk) == 0)
        def _():
            def arrived(group, carry):
                each_peer(
                    lambda step, peer: half_copy(
                        chunk * groups + group, step, peer, peer
                    ).wait_recv()
                )
                return carry

            lax.fori_loop(0, groups, arrived, 0)

        load = pltpu.make_async_copy(
            landed.at[:, :, pl.ds(batch * ROWS, ROWS)], halves, load_sem
        )
        load.start()
        load.wait()

        def one_pair(pair, carry):
            if group_rows % ROWS == 0:
                half = halves[:, :, pair].reshape(orbitals, orbitals)
            else:
                for origin in range(peers):
                    for group in range(groups):
                        packed[pl.ds((origin * groups + group) * group_rows, group_rows), :] = (
                            halves[origin, group, pair].astype(jnp.float32)
                        )
                half = packed[...].astype(jnp.bfloat16)
            full = jnp.dot(rotation_t[...], half, preferred_element_type=jnp.float32)
            index = lax.axis_index("ob") * pair_count + first_row(batch, me) + pair
            energy = eps_occ[lax.div(index, occupied)] + eps_occ[lax.rem(index, occupied)]
            divisor = energy - eps_first[...] - eps_vir[...].reshape(1, orbitals)
            full = full / divisor
            first = pl.multiple_of(pair * orbitals, orbitals)
            for strip in range(strips):
                spread[strip, pl.ds(first, orbitals), :] = full[
                    :, strip * LANES : (strip + 1) * LANES
                ]
            return carry

        lax.fori_loop(0, ROWS, one_pair, 0)

        @pl.when(batch >= 2)
        def _():
            each_peer(lambda step, peer: update_copy(batch - 2, step, peer, me).wait_send())

        def lay_out(orbital, carry):
            for strip in range(strips):
                column = pl.multiple_of(orbital * orbitals + strip * LANES, LANES)
                updates[slot, :, pl.ds(column, LANES)] = spread[
                    strip, pl.ds(orbital, ROWS, stride=orbitals), :
                ].astype(jnp.bfloat16)
            return carry

        lax.fori_loop(0, orbitals, lay_out, 0, unroll=8)
        each_peer(lambda step, peer: update_copy(batch, step, peer, me).start())
        own = pltpu.make_async_copy(
            updates.at[slot, :, pl.ds(pl.multiple_of(me * row_count, LANES), row_count)],
            out.at[pl.ds(first_row(batch, me), ROWS)],
            own_sem,
        )
        own.start()
        own.wait()
        return carry

    lax.fori_loop(0, batches, return_batch, 0)

    if gather:
        for chunk in range(chunks):
            each_peer(lambda step, peer: panel_copy(chunk, step, sibling, me, False).wait_send())
    for turn in range(max(0, turns - 2), turns):
        each_peer(lambda step, peer: half_copy(turn, step, peer, me).wait_send())
    for batch in range(max(0, batches - 2), batches):
        each_peer(lambda step, peer: update_copy(batch, step, peer, me).wait_send())

    def all_arrived(batch, carry):
        each_peer(lambda step, peer: update_copy(batch, step, peer, peer).wait_recv())
        return carry

    lax.fori_loop(0, batches, all_arrived, 0)


def copy_kernel(source, target, parts, in_sem, out_sem):
    count, rows, _ = parts.shape

    def read(part):
        return pltpu.make_async_copy(
            source.at[pl.ds(part * rows, rows)], parts.at[part], in_sem.at[part]
        )

    def write(part):
        return pltpu.make_async_copy(
            parts.at[part], target.at[pl.ds(part * rows, rows)], out_sem.at[part]
        )

    for part in range(count):
        read(part).start()
    for part in range(count):
        read(part).wait()
        write(part).start()
    for part in range(count):
        write(part).wait()


def shards(integrals, amplitudes, rotation, eps_occ, eps_vir):
    row_count, summed = integrals.shape
    depth, pair_count = amplitudes.shape
    orbitals = rotation.shape[0]
    peers = lax.axis_size("vp")
    per_owner = pair_count // peers
    first_rows = row_count // orbitals
    group_rows = ROWS if first_rows % ROWS == 0 else first_rows
    groups = first_rows // group_rows
    chunks = 2 if per_owner % (2 * ROWS) == 0 else 1
    chunk_pairs = per_owner // chunks
    width = peers * chunk_pairs
    batches = per_owner // ROWS
    turns = chunks * groups
    gather = depth % ROWS == 0 and peers % 2 == 0
    if not gather:
        amplitudes = lax.all_gather(amplitudes, "vp", axis=0, tiled=True)
        depth = summed
    bf16, f32 = jnp.bfloat16, jnp.float32
    vmem = pl.BlockSpec(memory_space=pltpu.VMEM)
    anywhere = pl.BlockSpec(memory_space=pl.ANY)
    spare = (LANES, LANES) if group_rows % ROWS == 0 else (orbitals, orbitals)
    flops = 2 * row_count * summed * pair_count + 4 * pair_count * row_count * orbitals
    result, _ = pl.pallas_call(
        functools.partial(ladder_kernel, peers, gather),
        out_shape=(
            jax.ShapeDtypeStruct((pair_count, row_count), bf16),
            jax.ShapeDtypeStruct((peers, groups, per_owner, group_rows, orbitals), bf16),
        ),
        in_specs=[
            anywhere,
            anywhere,
            vmem,
            pl.BlockSpec(memory_space=pltpu.SMEM),
            vmem,
        ],
        out_specs=(anywhere, anywhere),
        scratch_shapes=[
            pltpu.VMEM((chunks, summed // depth, depth, width), bf16),
            pltpu.VMEM((SLOTS, orbitals, summed), bf16),
            pltpu.VMEM(
                (orbitals // LANES, max(width * group_rows, ROWS * orbitals), LANES), f32
            ),
            pltpu.VMEM((2, width, group_rows, orbitals), bf16),
            pltpu.VMEM((peers, groups, ROWS, group_rows, orbitals), bf16),
            pltpu.VMEM((2, ROWS, orbitals * orbitals), bf16),
            pltpu.VMEM(spare, f32),
            pltpu.VMEM((orbitals, orbitals), bf16),
            pltpu.VMEM((orbitals, orbitals), f32),
            pltpu.SemaphoreType.DMA((chunks, peers)),
            pltpu.SemaphoreType.DMA((chunks, peers)),
            pltpu.SemaphoreType.DMA,
            pltpu.SemaphoreType.DMA((SLOTS,)),
            pltpu.SemaphoreType.DMA((2, peers)),
            pltpu.SemaphoreType.DMA((turns, peers)),
            pltpu.SemaphoreType.DMA,
            pltpu.SemaphoreType.DMA((2, peers)),
            pltpu.SemaphoreType.DMA((batches, peers)),
        ],
        cost_estimate=pl.CostEstimate(
            flops=flops, bytes_accessed=chunks * 2 * row_count * summed, transcendentals=0
        ),
        compiler_params=pltpu.CompilerParams(
            collective_id=0, has_side_effects=True, vmem_limit_bytes=60 * 1024 * 1024
        ),
    )(amplitudes, integrals, rotation, eps_occ, eps_vir)
    parts = pair_count // (2 * ROWS)
    return pl.pallas_call(
        copy_kernel,
        out_shape=jax.ShapeDtypeStruct(result.shape, bf16),
        in_specs=[anywhere],
        out_specs=anywhere,
        scratch_shapes=[
            pltpu.VMEM((parts, 2 * ROWS, row_count), bf16),
            pltpu.SemaphoreType.DMA((parts,)),
            pltpu.SemaphoreType.DMA((parts,)),
        ],
        cost_estimate=pl.CostEstimate(
            flops=0, bytes_accessed=4 * pair_count * row_count, transcendentals=0
        ),
        compiler_params=pltpu.CompilerParams(vmem_limit_bytes=60 * 1024 * 1024),
    )(result)


def solution(mesh):
    return jax.shard_map(
        shards,
        mesh=mesh,
        in_specs=(P("vp", None), P("vp", "ob"), P(), P(), P()),
        out_specs=P("ob", "vp"),
        check_vma=False,
    )
```
